32 devices in a mesh: shot: 2 (over x), depth: 2 (over core), lat: 8 (over z, y).
Axes of the slice: x: 2, y: 2, z: 4, core: 2. Of those that a mesh axis runs over, the one named last changes fastest.
Arguments:
- wavefields: bfloat16 [8, 4, 1024, 1024], P('shot', None, 'lat'), parts along dimension 0, may hold values from -12 to 12
- angular_freq: float32 [4], replicated, may hold values from 0.6 to 2.4
- base_slowness: float32 [2], replicated, may hold values from 0.7 to 0.9
- slow_table: float32 [2, 16], replicated, may hold values from 0.8 to 1.4
- correction_table: float32 [2, 16], replicated, may hold values from 0.05 to 0.2
- velocity_bins: int32 [2, 1024, 1024], P(None, 'lat'), may hold values from 0 to 15
- last_slab: int32 [4], replicated, may hold values from 1 to 2, as said below
Outputs:
- slab_image: bfloat16 [4, 1024, 1024], P(('shot', 'depth'), 'lat'), parts along dimension 0
- slab_fields: bfloat16 [4, 4, 4, 1024, 1024], P(('shot', 'depth'), None, None, 'lat'), parts along dimension 0
The draws below stay inside these ranges and needn't reach their ends.
There are 2 independent parts, one for each index of `shot`. The reference program is written for one: setup_inputs(seed, part) draws one part's arguments, and reference() takes and returns one part's arrays. A program takes and returns all parts, laid end to end along the dimension named above; an argument that names none is the same for every part. Nothing has to cross between parts.
Inputs may be any that keep to these rules, and one draw needn't show every extreme that they name: Frequency f is continued through slabs 0 to last_slab[f] - 1; some frequency goes through all 2 slabs and some stops after the first.
All inputs are finite; a program needn't handle non-finite values.
Results may differ from the reference program's by a relative error of at most 0.018.
Values may be sent and summed in bfloat16 or wider, within the bound.
A program may use at most 192 MiB of HBM per device.

```python
import math
import jax
import jax.numpy as jnp

NX = 1024
NY = 1024
FREQS = 4
BINS = 16
SLABS = 2


def draw_last_slab(key, part):
    first_key = jax.random.fold_in(key, 11)
    second_key = jax.random.fold_in(key, 12)
    values = jax.random.randint(first_key, (FREQS,), 1, SLABS + 1)
    shuffled = jax.random.permutation(second_key, FREQS)
    values = values.at[shuffled[0]].set(SLABS)
    values = values.at[shuffled[1]].set(1)
    return values.astype(jnp.int32)


def place_ends(result, rng, low, high):
    extent = result.shape
    index_at = [jax.random.randint(jax.random.fold_in(rng, axis), (), 0, extent[axis]) for axis in range(len(extent))]
    result = result.at[tuple(index_at)].set(low)
    longest = extent.index(max(extent))
    index_at[longest] = (index_at[longest] + 1) % extent[longest]
    return result.at[tuple(index_at)].set(high)


def block_levels(rng, dims, split, least, top_value):
    def one(axis_at, shards_of):
        draws = jax.random.uniform(jax.random.fold_in(jax.random.fold_in(rng, 6), axis_at), (shards_of,), jnp.float32, least / len(split), top_value / len(split))
        return jnp.repeat(jnp.exp(draws), dims[axis_at] // shards_of).reshape((-1,) + (1,) * (len(dims) - axis_at - 1))

    factor_of = one(*split[0])
    for cut in split[1:]:
        factor_of = factor_of * one(*cut)
    return factor_of


def gaussian(stream_key, shape, spread, limit, shards=(), kind=jnp.bfloat16):
    values = spread * jax.random.normal(stream_key, shape, jnp.float32)
    if shards:
        values = values * block_levels(stream_key, shape, shards, -0.22, 0.18)
    return jnp.clip(values, -limit, limit).astype(kind)


def setup_inputs(seed: int = 0, part: int = 0) -> dict:
    splits = jax.random.split(jax.random.key(seed), 8)
    part_splits = jax.random.split(jax.random.fold_in(splits[7], part), 8)
    return {
        "wavefields": gaussian(part_splits[0], (FREQS, 4, NX, NY), 2.0, 12.0, ((2, 8),)),
        "angular_freq": jnp.clip(jnp.exp(jax.random.uniform(splits[1], (FREQS,), jnp.float32, math.log(0.6), math.log(2.4))), 0.6, 2.4),
        "base_slowness": jnp.clip(jax.random.uniform(splits[2], (SLABS,), jnp.float32, 0.7, 0.9), 0.7, 0.9),
        "slow_table": jnp.clip(jax.random.uniform(splits[3], (SLABS, BINS), jnp.float32, 0.8, 1.4), 0.8, 1.4),
        "correction_table": jnp.clip(jax.random.uniform(splits[4], (SLABS, BINS), jnp.float32, 0.05, 0.2), 0.05, 0.2),
        "velocity_bins": place_ends(jax.random.randint(splits[5], (SLABS, NX, NY), 0, BINS), jax.random.fold_in(splits[5], 1), 0, BINS - 1).astype(jnp.int32),
        "last_slab": draw_last_slab(jax.random.fold_in(splits[7], 71), part),
    }


depth_step = 1.0

def transform_tables(row_indices, column_indices, period):
    product = row_indices[:, None] * column_indices[None, :] % period
    angle = 2.0 * jnp.pi / period * product.astype(jnp.float32)
    return (jnp.cos(angle).astype(jnp.bfloat16), jnp.sin(angle).astype(jnp.bfloat16))

def wavenumber(indices, period):
    signed = jnp.where(indices < period // 2, indices, indices - period)
    return 2.0 * jnp.pi / period * signed.astype(jnp.float32)

def forward_pair(first_part, second_part):
    return jnp.stack([first_part[0] + second_part[1], first_part[1] - second_part[0], first_part[2] + second_part[3], first_part[3] - second_part[2]])

def inverse_pair(first_part, second_part):
    return jnp.stack([first_part[0] - second_part[1], first_part[1] + second_part[0], first_part[2] - second_part[3], first_part[3] + second_part[2]])

def rotate(planes, cosine, sine):
    return jnp.stack([planes[0] * cosine + planes[1] * sine, planes[1] * cosine - planes[0] * sine, planes[2] * cosine - planes[3] * sine, planes[3] * cosine + planes[2] * sine])

def laplace(padded, planes):
    vertical = padded[:, :-2] + padded[:, 2:]
    sideways = jnp.pad(planes, ((0, 0), (0, 0), (1, 1)))
    return vertical + sideways[:, :, :-2] + sideways[:, :, 2:] - 4.0 * planes

def correct(planes, coefficient, laplacian):
    return jnp.stack([planes[0] + coefficient * laplacian[1], planes[1] - coefficient * laplacian[0], planes[2] - coefficient * laplacian[3], planes[3] + coefficient * laplacian[2]])

def cross_term(planes):
    return planes[0] * planes[2] + planes[1] * planes[3]

def phase_factor(angular, base, row_wave, column_wave):
    vertical_sq = (angular * base) ** 2 - row_wave ** 2 - column_wave ** 2
    magnitude = jnp.sqrt(jnp.abs(vertical_sq))
    moving = vertical_sq >= 0.0
    cosine = jnp.where(moving, jnp.cos(depth_step * magnitude), jnp.exp(-depth_step * magnitude))
    sine = jnp.where(moving, jnp.sin(depth_step * magnitude), 0.0)
    return (cosine, sine)

def propagate(planes, angular, base, slowness, coefficient, row_cosine, row_sine, column_cosine, column_sine):
    wide = planes.astype(jnp.float32)
    first_part = jnp.einsum('qxy,yk->qxk', wide, column_cosine.astype(jnp.float32))
    second_part = jnp.einsum('qxy,yk->qxk', wide, column_sine.astype(jnp.float32))
    row_spectrum = forward_pair(first_part, second_part).astype(jnp.bfloat16)
    wide = row_spectrum.astype(jnp.float32)
    first_part = jnp.einsum('qxy,xk->qky', wide, row_cosine.astype(jnp.float32))
    second_part = jnp.einsum('qxy,xk->qky', wide, row_sine.astype(jnp.float32))
    spectrum = forward_pair(first_part, second_part)
    row_wave = wavenumber(jnp.arange(NX, dtype=jnp.int32), NX)[:, None]
    column_wave = wavenumber(jnp.arange(NY, dtype=jnp.int32), NY)[None, :]
    cosine, sine = phase_factor(angular, base, row_wave, column_wave)
    shifted = rotate(spectrum, cosine, sine).astype(jnp.bfloat16)
    wide = shifted.astype(jnp.float32)
    first_part = jnp.einsum('qky,xk->qxy', wide, row_cosine.astype(jnp.float32))
    second_part = jnp.einsum('qky,xk->qxy', wide, row_sine.astype(jnp.float32))
    column_field = inverse_pair(first_part, second_part).astype(jnp.bfloat16)
    wide = column_field.astype(jnp.float32)
    first_part = jnp.einsum('qxy,yk->qxk', wide, column_cosine.astype(jnp.float32))
    second_part = jnp.einsum('qxy,yk->qxk', wide, column_sine.astype(jnp.float32))
    restored = inverse_pair(first_part, second_part) / (NX * NY)
    turn = depth_step * angular * (slowness - base)
    turned = rotate(restored, jnp.cos(turn), jnp.sin(turn))
    padded = jnp.pad(turned, ((0, 0), (1, 1), (0, 0)))
    return correct(turned, coefficient, laplace(padded, turned))

def reference(wavefields, angular_freq, base_slowness, slow_table, correction_table, velocity_bins, last_slab):
    row_indices = jnp.arange(NX, dtype=jnp.int32)
    column_indices = jnp.arange(NY, dtype=jnp.int32)
    row_cosine, row_sine = transform_tables(row_indices, row_indices, NX)
    column_cosine, column_sine = transform_tables(column_indices, column_indices, NY)
    current = wavefields
    images = []
    outputs = []
    for slab_index in range(SLABS):
        bins_here = velocity_bins[slab_index]
        slowness = slow_table[slab_index][bins_here]
        coefficient = correction_table[slab_index][bins_here]
        image_sum = jnp.zeros((NX, NY), jnp.float32)
        masked_list = []
        for frequency in range(FREQS):
            corrected = propagate(current[frequency], angular_freq[frequency], base_slowness[slab_index], slowness, coefficient, row_cosine, row_sine, column_cosine, column_sine)
            active = slab_index < last_slab[frequency]
            image_sum = image_sum + jnp.where(active, cross_term(corrected), 0.0)
            masked_list.append(jnp.where(active, corrected, 0.0).astype(jnp.bfloat16))
        current = jnp.stack(masked_list)
        images.append(image_sum.astype(jnp.bfloat16))
        outputs.append(current)
    return (jnp.stack(images), jnp.stack(outputs))
```

```python
import functools

import jax
import jax.numpy as jnp
import ml_dtypes
import numpy as np
from jax import lax
from jax.experimental import pallas as pl
from jax.experimental.pallas import tpu as pltpu
from jax.sharding import PartitionSpec as P

depth_step = 1.0
LANES = 128
MESH = pl.DeviceIdType.MESH
bf16 = jnp.bfloat16
f32 = jnp.float32

COS_TERMS = (1.0, -1 / 2, 1 / 24, -1 / 720, 1 / 40320, -1 / 3628800, 1 / 479001600)
SIN_TERMS = (1.0, -1 / 6, 1 / 120, -1 / 5040, 1 / 362880, -1 / 39916800, 1 / 6227020800)


def series(terms, square):
    total = jnp.full_like(square, terms[-1])
    for term in terms[-2::-1]:
        total = total * square + term
    return total


def wave_tables(period):
    index = np.arange(period, dtype=np.int64)
    product = (index[:, None] * index[None, :]) % period
    angle = 2.0 * np.pi / period * product
    return (np.cos(angle).astype(ml_dtypes.bfloat16), np.sin(angle).astype(ml_dtypes.bfloat16))


def forward_blocks(cosine, sine, count, padded):
    period = cosine.shape[0]
    width = period // count
    table = np.zeros((count, period, 2, padded), ml_dtypes.bfloat16)
    for part, values in enumerate((cosine, sine)):
        table[:, :, part, :width] = values.reshape(period, count, width).transpose(1, 0, 2)
    return table.reshape(count, period, 2 * padded)


def inverse_blocks(cosine, sine, count, padded):
    period = cosine.shape[0]
    width = period // count
    blocks = period // LANES
    table = np.zeros((blocks, count, padded, 2, LANES), ml_dtypes.bfloat16)
    for part, values in enumerate((cosine, sine)):
        table[:, :, :width, part] = values.reshape(count, width, blocks, LANES).transpose(2, 0, 1, 3)
    return table.reshape(blocks, count * padded, 2 * LANES)


def row_blocks(cosine, sine, count):
    period = cosine.shape[0]
    rows = period // count
    both = np.stack([cosine.reshape(count, rows, period), sine.reshape(count, rows, period)], axis=1)
    return both.reshape(count, 2 * rows, period)


def migrate(
    sizes,
    perm,
    angular,
    bases,
    slow_table,
    corr_table,
    fields_hbm,
    bins_hbm,
    fwd_hbm,
    row_hbm,
    inv_hbm,
    out_hbm,
    fields,
    bins,
    fwd,
    rowt,
    inv,
    slow,
    coef,
    first,
    out1,
    land1,
    shifted,
    out2,
    land2,
    turned,
    halo_out,
    halo_in,
    done,
    load_sem,
    send1,
    recv1,
    send2,
    recv2,
    halo_send,
    halo_recv,
    keep_sem,
    pair_send,
    pair_recv,
):
    freqs, units, lat, rows, columns, width, padded, bin_count = sizes
    total_rows = rows * lat
    me = lax.axis_index("lat")
    section = lax.axis_index("depth")
    sign = jnp.where(section == 0, -1.0, 1.0).astype(f32)
    y_blocks = columns // LANES

    loads = [
        pltpu.make_async_copy(fwd_hbm, fwd, load_sem.at[0]),
        pltpu.make_async_copy(fields_hbm.at[:, pl.ds(2 * section, 2)], fields, load_sem.at[1]),
        pltpu.make_async_copy(row_hbm, rowt, load_sem.at[2]),
        pltpu.make_async_copy(bins_hbm, bins, load_sem.at[3]),
        pltpu.make_async_copy(inv_hbm, inv, load_sem.at[4]),
    ]
    for load in loads:
        load.start()

    halo_out[...] = jnp.zeros_like(halo_out)

    @pl.when(me == 0)
    def _():
        halo_in[:, 0] = jnp.zeros((units, 8, columns), f32)

    @pl.when(me == lat - 1)
    def _():
        halo_in[:, 1] = jnp.zeros((units, 8, columns), f32)

    barrier = pltpu.get_barrier_semaphore()

    @pl.loop(1, lat)
    def _(step):
        pl.semaphore_signal(
            barrier, inc=1, device_id={"lat": lax.rem(me + step, lat)}, device_id_type=MESH
        )

    pl.semaphore_signal(barrier, inc=1, device_id={"depth": 1 - section}, device_id_type=MESH)
    pl.semaphore_wait(barrier, lat)
    loads[0].wait()
    loads[1].wait()

    def spot(index):
        return pl.ds(pl.multiple_of(index * rows, rows), rows)

    def lane_spot(index):
        return pl.ds(pl.multiple_of(index * padded, padded), padded)

    def copy1(unit, step, peer):
        return pltpu.make_async_remote_copy(
            src_ref=out1.at[unit, step],
            dst_ref=land1.at[unit, spot(me)],
            send_sem=send1.at[unit],
            recv_sem=recv1.at[unit],
            device_id={"lat": peer},
            device_id_type=MESH,
        )

    def copy2(unit, step, peer):
        return pltpu.make_async_remote_copy(
            src_ref=out2.at[unit, step],
            dst_ref=land2.at[unit, :, lane_spot(me)],
            send_sem=send2.at[unit],
            recv_sem=recv2.at[unit],
            device_id={"lat": peer},
            device_id_type=MESH,
        )

    def halo_up(unit):
        return pltpu.make_async_remote_copy(
            src_ref=halo_out.at[unit, 0],
            dst_ref=halo_in.at[unit, 1],
            send_sem=halo_send.at[unit, 0],
            recv_sem=halo_recv.at[unit, 1],
            device_id={"lat": jnp.maximum(me - 1, 0)},
            device_id_type=MESH,
        )

    def halo_down(unit):
        return pltpu.make_async_remote_copy(
            src_ref=halo_out.at[unit, 1],
            dst_ref=halo_in.at[unit, 0],
            send_sem=halo_send.at[unit, 1],
            recv_sem=halo_recv.at[unit, 0],
            device_id={"lat": jnp.minimum(me + 1, lat - 1)},
            device_id_type=MESH,
        )

    def pair_copy(unit):
        return pltpu.make_async_remote_copy(
            src_ref=done.at[unit],
            dst_ref=out_hbm.at[section, unit],
            send_sem=pair_send.at[unit],
            recv_sem=pair_recv.at[unit],
            device_id={"depth": 1 - section},
            device_id_type=MESH,
        )

    def keep_copy(unit):
        return pltpu.make_async_copy(done.at[unit], out_hbm.at[section, unit], keep_sem.at[unit])

    def scalars(unit):
        slab = unit // freqs
        slot = unit - slab * freqs
        return slab, angular[perm[slot]], bases[slab]

    def row_forward(unit):
        @pl.when(unit < freqs)
        def _():
            first[...] = fields[perm[unit]].reshape(2 * rows, columns)

        @pl.when(unit >= freqs)
        def _():
            first[...] = done[unit - freqs].reshape(2 * rows, columns)

        @pl.loop(0, lat)
        def _(step):
            peer = lax.rem(me + step + 1, lat)
            part = jnp.dot(first[...], fwd[peer], preferred_element_type=f32)
            real = part[:rows, :padded] + part[rows:, padded:]
            imag = part[rows:, :padded] - part[:rows, padded:]

            @pl.when(step < lat - 1)
            def _():
                out1[unit, step, :, :padded] = real.astype(bf16)
                out1[unit, step, :, padded:] = imag.astype(bf16)
                copy1(unit, step, peer).start()

            @pl.when(step == lat - 1)
            def _():
                land1[unit, spot(me), :padded] = real.astype(bf16)
                land1[unit, spot(me), padded:] = imag.astype(bf16)

    def column_phase(unit):
        whole = land1.at[unit, pl.ds(0, (lat - 1) * rows)]
        pltpu.make_async_copy(whole, whole, recv1.at[unit]).wait()
        _, speed, base = scalars(unit)
        limit = (speed * base) ** 2
        lane = lax.broadcasted_iota(jnp.int32, (1, padded), 1) + me * width
        lane = jnp.where(lane < columns // 2, lane, lane - columns)
        column_wave = (2.0 * np.pi / columns) * lane.astype(f32)
        left = limit - column_wave * column_wave

        @pl.loop(0, lat)
        def _(block):
            part = jnp.dot(rowt[block], land1[unit], preferred_element_type=f32)
            real = part[:rows, :padded] + part[rows:, padded:]
            imag = part[:rows, padded:] - part[rows:, :padded]
            index = lax.broadcasted_iota(jnp.int32, (rows, 1), 0) + block * rows
            index = jnp.where(index < total_rows // 2, index, index - total_rows)
            row_wave = (2.0 * np.pi / total_rows) * index.astype(f32)
            square = left - row_wave * row_wave
            root = jnp.sqrt(jnp.abs(square)) * depth_step
            moving = square >= 0.0
            cosine = jnp.where(moving, series(COS_TERMS, square), jnp.exp(-root))
            sine = jnp.where(moving, root * series(SIN_TERMS, square), 0.0) * sign
            shifted[spot(block), :padded] = (real * cosine - imag * sine).astype(bf16)
            shifted[spot(block), padded:] = (imag * cosine + real * sine).astype(bf16)

        @pl.loop(0, lat)
        def _(step):
            peer = lax.rem(me + step + 1, lat)
            part = jnp.dot(rowt[peer], shifted[...], preferred_element_type=f32)
            real = part[:rows, :padded] - part[rows:, padded:]
            imag = part[:rows, padded:] + part[rows:, :padded]

            @pl.when(step < lat - 1)
            def _():
                out2[unit, step, :rows] = real.astype(bf16)
                out2[unit, step, rows:] = imag.astype(bf16)
                copy2(unit, step, peer).start()

            @pl.when(step == lat - 1)
            def _():
                land2[unit, :rows, lane_spot(me)] = real.astype(bf16)
                land2[unit, rows:, lane_spot(me)] = imag.astype(bf16)

    def row_inverse(unit):
        whole = land2.at[unit, :, pl.ds(0, (lat - 1) * padded)]
        pltpu.make_async_copy(whole, whole, recv2.at[unit]).wait()
        slab, speed, base = scalars(unit)
        scale = 1.0 / (total_rows * columns)
        slot = lax.rem(unit, 2)

        @pl.loop(0, y_blocks)
        def _(block):
            cols = pl.ds(pl.multiple_of(block * LANES, LANES), LANES)
            part = jnp.dot(land2[unit], inv[block], preferred_element_type=f32)
            real = part[:rows, :LANES] - part[rows:, LANES:]
            imag = part[rows:, :LANES] + part[:rows, LANES:]
            turn = depth_step * speed * (slow[slab, :, cols] - base)
            square = turn * turn
            cosine = series(COS_TERMS, square) * scale
            sine = turn * series(SIN_TERMS, square) * (sign * scale)
            new_real = real * cosine - imag * sine
            new_imag = imag * cosine + real * sine
            turned[slot, 0, 8 : 8 + rows, cols] = new_real
            turned[slot, 1, 8 : 8 + rows, cols] = new_imag
            halo_out[unit, 0, 0:1, cols] = new_real[0:1]
            halo_out[unit, 0, 1:2, cols] = new_imag[0:1]
            halo_out[unit, 1, 0:1, cols] = new_real[rows - 1 : rows]
            halo_out[unit, 1, 1:2, cols] = new_imag[rows - 1 : rows]

        @pl.when(me > 0)
        def _():
            halo_up(unit).start()

        @pl.when(me < lat - 1)
        def _():
            halo_down(unit).start()

    def finish(unit):
        @pl.when(me > 0)
        def _():
            halo_down(unit).wait_recv()

        @pl.when(me < lat - 1)
        def _():
            halo_up(unit).wait_recv()

        slab = unit // freqs
        slot = lax.rem(unit, 2)
        for plane in range(2):
            turned[slot, plane, 7:8] = halo_in[unit, 0, plane : plane + 1]
            turned[slot, plane, 8 + rows : 9 + rows] = halo_in[unit, 1, plane : plane + 1]
        lane = lax.broadcasted_iota(jnp.int32, (16, columns), 1)
        for start in range(0, rows, 16):
            middle, laps = [], []
            for plane in range(2):
                here = turned[slot, plane, 8 + start : 24 + start]
                above = turned[slot, plane, 7 + start : 23 + start]
                below = turned[slot, plane, 9 + start : 25 + start]
                left = jnp.where(lane == 0, 0.0, pltpu.roll(here, 1, 1))
                right = jnp.where(lane == columns - 1, 0.0, pltpu.roll(here, columns - 1, 1))
                middle.append(here)
                laps.append(above + below + left + right - 4.0 * here)
            weight = coef[slab, start : start + 16] * sign
            done[unit, 0, start : start + 16] = (middle[0] - weight * laps[1]).astype(bf16)
            done[unit, 1, start : start + 16] = (middle[1] + weight * laps[0]).astype(bf16)
        keep_copy(unit).start()
        pair_copy(unit).start()

    def look_up():
        @pl.loop(0, (columns // LANES) * 2)
        def _(index):
            slab = index // y_blocks
            block = index - slab * y_blocks
            cols = pl.ds(pl.multiple_of(block * LANES, LANES), LANES)
            here = bins[slab, :, cols]
            found_slow = jnp.zeros((rows, LANES), f32)
            found_coef = jnp.zeros((rows, LANES), f32)
            for level in range(bin_count):
                match = here == level
                found_slow = jnp.where(match, slow_table[slab, level], found_slow)
                found_coef = jnp.where(match, corr_table[slab, level], found_coef)
            slow[slab, :, cols] = found_slow
            coef[slab, :, cols] = found_coef

    @pl.loop(0, units + 3)
    def _(tick):
        @pl.when(tick >= 3)
        def _():
            finish(tick - 3)

        @pl.when(tick < units)
        def _():
            row_forward(tick)

        @pl.when(tick == 0)
        def _():
            loads[2].wait()
            loads[3].wait()
            loads[4].wait()
            look_up()

        @pl.when((tick >= 1) & (tick < units + 1))
        def _():
            column_phase(tick - 1)

        @pl.when((tick >= 2) & (tick < units + 2))
        def _():
            row_inverse(tick - 2)

    @pl.loop(0, units)
    def _(unit):
        sent1 = out1.at[unit, pl.ds(0, lat - 1)]
        pltpu.make_async_copy(sent1, sent1, send1.at[unit]).wait()
        sent2 = out2.at[unit, pl.ds(0, lat - 1)]
        pltpu.make_async_copy(sent2, sent2, send2.at[unit]).wait()

        @pl.when(me > 0)
        def _():
            halo_up(unit).wait_send()

        @pl.when(me < lat - 1)
        def _():
            halo_down(unit).wait_send()

        keep_copy(unit).wait()
        pltpu.make_async_remote_copy(
            src_ref=done.at[unit],
            dst_ref=out_hbm.at[1 - section, unit],
            send_sem=pair_send.at[unit],
            recv_sem=pair_recv.at[unit],
            device_id={"depth": 1 - section},
            device_id_type=MESH,
        ).wait()


def collect(freqs, picks, live, moved, image, fields, total):
    freq = pl.program_id(1)

    @pl.when(freq == 0)
    def _():
        total[...] = jnp.zeros_like(total)

    @pl.when(live[freq] > 0)
    def _():
        fields[0, 0, 0:2] = moved[0, 0]
        fields[0, 0, 2:4] = moved[1, 0]
        source = moved[0, 0].astype(f32)
        receiver = moved[1, 0].astype(f32)
        total[...] += source[0] * receiver[0] + source[1] * receiver[1]

    @pl.when(live[freq] == 0)
    def _():
        fields[...] = jnp.zeros_like(fields)

    @pl.when(freq == freqs - 1)
    def _():
        image[0] = total[...].astype(image.dtype)


def per_device(
    fwd_table,
    row_table,
    inv_table,
    wavefields,
    angular_freq,
    base_slowness,
    slow_table,
    correction_table,
    velocity_bins,
    last_slab,
):
    freqs, _, rows, columns = wavefields.shape
    slabs, bin_count = slow_table.shape
    lat = lax.axis_size("lat")
    section = lax.axis_index("depth")
    width = columns // lat
    padded = max(LANES, width)
    continued = last_slab > 1
    order = jnp.arange(freqs, dtype=jnp.int32)
    key = jnp.where(continued, order, order + freqs)
    rank = jnp.sum((key[None, :] < key[:, None]).astype(jnp.int32), axis=1)
    perm = jnp.sum(jnp.where(rank[None, :] == order[:, None], order[None, :], 0), axis=1)
    count = jnp.sum(continued.astype(jnp.int32))
    live = (section < last_slab).astype(jnp.int32)

    def branch(number):
        units = freqs + number
        sizes = (freqs, units, lat, rows, columns, width, padded, bin_count)
        smem = pl.BlockSpec(memory_space=pltpu.SMEM)
        hbm = pl.BlockSpec(memory_space=pl.ANY)
        chunk = (units, lat - 1, rows, 2 * padded)
        moved = pl.pallas_call(
            functools.partial(migrate, sizes),
            out_shape=jax.ShapeDtypeStruct((2, units, 2, rows, columns), bf16),
            in_specs=[smem] * 5 + [hbm] * 5,
            out_specs=hbm,
            scratch_shapes=[
                pltpu.VMEM((freqs, 2, rows, columns), bf16),
                pltpu.VMEM((slabs, rows, columns), jnp.int32),
                pltpu.VMEM(fwd_table.shape, bf16),
                pltpu.VMEM(row_table.shape, bf16),
                pltpu.VMEM(inv_table.shape, bf16),
                pltpu.VMEM((slabs, rows, columns), f32),
                pltpu.VMEM((slabs, rows, columns), f32),
                pltpu.VMEM((2 * rows, columns), bf16),
                pltpu.VMEM(chunk, bf16),
                pltpu.VMEM((units, rows * lat, 2 * padded), bf16),
                pltpu.VMEM((rows * lat, 2 * padded), bf16),
                pltpu.VMEM((units, lat - 1, 2 * rows, padded), bf16),
                pltpu.VMEM((units, 2 * rows, lat * padded), bf16),
                pltpu.VMEM((2, 2, rows + 16, columns), f32),
                pltpu.VMEM((units, 2, 8, columns), f32),
                pltpu.VMEM((units, 2, 8, columns), f32),
                pltpu.VMEM((units, 2, rows, columns), bf16),
                pltpu.SemaphoreType.DMA((5,)),
                pltpu.SemaphoreType.DMA((units,)),
                pltpu.SemaphoreType.DMA((units,)),
                pltpu.SemaphoreType.DMA((units,)),
                pltpu.SemaphoreType.DMA((units,)),
                pltpu.SemaphoreType.DMA((units, 2)),
                pltpu.SemaphoreType.DMA((units, 2)),
                pltpu.SemaphoreType.DMA((units,)),
                pltpu.SemaphoreType.DMA((units,)),
                pltpu.SemaphoreType.DMA((units,)),
            ],
            compiler_params=pltpu.CompilerParams(
                collective_id=number - 1, has_side_effects=True, vmem_limit_bytes=62 * 2**20
            ),
            name=f"migrate_{units}",
        )(
            perm,
            angular_freq,
            base_slowness,
            slow_table,
            correction_table,
            wavefields,
            velocity_bins,
            fwd_table,
            row_table,
            inv_table,
        )
        picks = jnp.where(section == 0, rank, jnp.minimum(freqs + rank, units - 1))
        tile = min(rows, 32)
        return pl.pallas_call(
            functools.partial(collect, freqs),
            out_shape=(
                jax.ShapeDtypeStruct((1, rows, columns), bf16),
                jax.ShapeDtypeStruct((1, freqs, 4, rows, columns), bf16),
            ),
            grid_spec=pltpu.PrefetchScalarGridSpec(
                num_scalar_prefetch=2,
                grid=(rows // tile, freqs),
                in_specs=[
                    pl.BlockSpec((2, 1, 2, tile, columns), lambda r, f, picks, live: (0, picks[f], 0, r, 0))
                ],
                out_specs=[
                    pl.BlockSpec((1, tile, columns), lambda r, f, picks, live: (0, r, 0)),
                    pl.BlockSpec((1, 1, 4, tile, columns), lambda r, f, picks, live: (0, f, 0, r, 0)),
                ],
                scratch_shapes=[pltpu.VMEM((tile, columns), f32)],
            ),
            name=f"collect_{units}",
        )(picks, live, moved)

    picked = jnp.clip(count - 1, 0, freqs - 2)
    return lax.switch(picked, [functools.partial(branch, number) for number in range(1, freqs)])


def solution(mesh):
    lat = mesh.shape["lat"]
    in_specs = (
        P(),
        P(),
        P(),
        P("shot", None, "lat", None),
        P(),
        P(),
        P(),
        P(),
        P(None, "lat", None),
        P(),
    )
    out_specs = (P(("shot", "depth"), "lat", None), P(("shot", "depth"), None, None, "lat", None))
    body = jax.shard_map(
        per_device, mesh=mesh, in_specs=in_specs, out_specs=out_specs, check_vma=False
    )

    def run(wavefields, *rest):
        total_rows, columns = wavefields.shape[2:]
        padded = max(LANES, columns // lat)
        cosine_x, sine_x = wave_tables(total_rows)
        cosine_y, sine_y = wave_tables(columns)
        return body(
            jnp.asarray(forward_blocks(cosine_y, sine_y, lat, padded)),
            jnp.asarray(row_blocks(cosine_x, sine_x, lat)),
            jnp.asarray(inverse_blocks(cosine_y, sine_y, lat, padded)),
            wavefields,
            *rest,
        )

    return run
```

```python
import functools

import jax
import jax.numpy as jnp
import ml_dtypes
import numpy as np
from jax import lax
from jax.experimental import pallas as pl
from jax.experimental.pallas import tpu as pltpu
from jax.sharding import PartitionSpec as P

depth_step = 1.0
LANES = 128
MESH = pl.DeviceIdType.MESH
bf16 = jnp.bfloat16
f32 = jnp.float32

COS_TERMS = (1.0, -1 / 2, 1 / 24, -1 / 720, 1 / 40320, -1 / 3628800, 1 / 479001600)
SIN_TERMS = (1.0, -1 / 6, 1 / 120, -1 / 5040, 1 / 362880, -1 / 39916800, 1 / 6227020800)


def series(terms, square):
    total = jnp.full_like(square, terms[-1])
    for term in terms[-2::-1]:
        total = total * square + term
    return total


def wave_tables(period):
    index = np.arange(period, dtype=np.int64)
    product = (index[:, None] * index[None, :]) % period
    angle = 2.0 * np.pi / period * product
    return (np.cos(angle).astype(ml_dtypes.bfloat16), np.sin(angle).astype(ml_dtypes.bfloat16))


def forward_blocks(cosine, sine, count, padded):
    period = cosine.shape[0]
    width = period // count
    table = np.zeros((count, period, 2, padded), ml_dtypes.bfloat16)
    for part, values in enumerate((cosine, sine)):
        table[:, :, part, :width] = values.reshape(period, count, width).transpose(1, 0, 2)
    return table.reshape(count, period, 2 * padded)


def inverse_blocks(cosine, sine, count, padded):
    period = cosine.shape[0]
    width = period // count
    blocks = period // LANES
    table = np.zeros((blocks, count, padded, 2, LANES), ml_dtypes.bfloat16)
    for part, values in enumerate((cosine, sine)):
        table[:, :, :width, part] = values.reshape(count, width, blocks, LANES).transpose(2, 0, 1, 3)
    return table.reshape(blocks, count * padded, 2 * LANES)


def group_of(lat, rows):
    group = max(1, min(lat, 1024 // (2 * rows)))
    while lat % group:
        group -= 1
    return group


def row_blocks(cosine, sine, count):
    period = cosine.shape[0]
    rows = period // count
    both = np.stack([cosine.reshape(count, rows, period), sine.reshape(count, rows, period)], axis=1)
    group = group_of(count, rows)
    return both.reshape(count // group, group * 2 * rows, period)


def migrate(
    sizes,
    perm,
    angular,
    bases,
    slow_table,
    corr_table,
    fields_hbm,
    bins_hbm,
    fwd_hbm,
    row_hbm,
    inv_hbm,
    out_hbm,
    fields,
    bins,
    fwd,
    rowt,
    inv,
    slow,
    coef,
    first,
    out1,
    land1,
    shifted,
    out2,
    land2,
    turned,
    halo_out,
    halo_in,
    done,
    load_sem,
    send1,
    recv1,
    send2,
    recv2,
    halo_send,
    halo_recv,
    keep_sem,
    pair_send,
    pair_recv,
):
    freqs, units, lat, rows, columns, width, padded, bin_count = sizes
    total_rows = rows * lat
    group = group_of(lat, rows)
    me = lax.axis_index("lat")
    section = lax.axis_index("depth")
    sign = jnp.where(section == 0, -1.0, 1.0).astype(f32)
    y_blocks = columns // LANES

    loads = [
        pltpu.make_async_copy(fwd_hbm, fwd, load_sem.at[0]),
        pltpu.make_async_copy(fields_hbm.at[:, pl.ds(2 * section, 2)], fields, load_sem.at[1]),
        pltpu.make_async_copy(row_hbm, rowt, load_sem.at[2]),
        pltpu.make_async_copy(bins_hbm, bins, load_sem.at[3]),
        pltpu.make_async_copy(inv_hbm, inv, load_sem.at[4]),
    ]
    for load in loads:
        load.start()

    halo_out[...] = jnp.zeros_like(halo_out)

    @pl.when(me == 0)
    def _():
        halo_in[:, 0] = jnp.zeros((units, 8, columns), f32)

    @pl.when(me == lat - 1)
    def _():
        halo_in[:, 1] = jnp.zeros((units, 8, columns), f32)

    barrier = pltpu.get_barrier_semaphore()

    @pl.loop(1, lat)
    def _(step):
        pl.semaphore_signal(
            barrier, inc=1, device_id={"lat": lax.rem(me + step, lat)}, device_id_type=MESH
        )

    pl.semaphore_signal(barrier, inc=1, device_id={"depth": 1 - section}, device_id_type=MESH)
    pl.semaphore_wait(barrier, lat)
    loads[0].wait()
    loads[1].wait()

    def spot(index):
        return pl.ds(pl.multiple_of(index * rows, rows), rows)

    def lane_spot(index):
        return pl.ds(pl.multiple_of(index * padded, padded), padded)

    def copy1(unit, peer):
        return pltpu.make_async_remote_copy(
            src_ref=out1.at[unit, peer],
            dst_ref=land1.at[unit, spot(me)],
            send_sem=send1.at[unit],
            recv_sem=recv1.at[unit],
            device_id={"lat": peer},
            device_id_type=MESH,
        )

    def copy2(unit, peer):
        return pltpu.make_async_remote_copy(
            src_ref=out2.at[unit, peer],
            dst_ref=land2.at[unit, :, lane_spot(me)],
            send_sem=send2.at[unit],
            recv_sem=recv2.at[unit],
            device_id={"lat": peer},
            device_id_type=MESH,
        )

    def halo_up(unit):
        return pltpu.make_async_remote_copy(
            src_ref=halo_out.at[unit, 0],
            dst_ref=halo_in.at[unit, 1],
            send_sem=halo_send.at[unit, 0],
            recv_sem=halo_recv.at[unit, 1],
            device_id={"lat": jnp.maximum(me - 1, 0)},
            device_id_type=MESH,
        )

    def halo_down(unit):
        return pltpu.make_async_remote_copy(
            src_ref=halo_out.at[unit, 1],
            dst_ref=halo_in.at[unit, 0],
            send_sem=halo_send.at[unit, 1],
            recv_sem=halo_recv.at[unit, 0],
            device_id={"lat": jnp.minimum(me + 1, lat - 1)},
            device_id_type=MESH,
        )

    def pair_copy(unit):
        return pltpu.make_async_remote_copy(
            src_ref=done.at[unit],
            dst_ref=out_hbm.at[section, unit],
            send_sem=pair_send.at[unit],
            recv_sem=pair_recv.at[unit],
            device_id={"depth": 1 - section},
            device_id_type=MESH,
        )

    def keep_copy(unit):
        return pltpu.make_async_copy(done.at[unit], out_hbm.at[section, unit], keep_sem.at[unit])

    def scalars(unit):
        slab = unit // freqs
        slot = unit - slab * freqs
        return slab, angular[perm[slot]], bases[slab]

    def row_forward(unit):
        @pl.when(unit < freqs)
        def _():
            first[...] = fields[perm[unit]].reshape(2 * rows, columns)

        @pl.when(unit >= freqs)
        def _():
            first[...] = done[unit - freqs].reshape(2 * rows, columns)

        @pl.loop(0, lat // 2)
        def _(step):
            peers = [lax.rem(me + 2 * step + shift, lat) for shift in (1, 2)]
            for peer in peers:
                part = jnp.dot(first[...], fwd[peer], preferred_element_type=f32)
                real = part[:rows, :padded] + part[rows:, padded:]
                imag = part[rows:, :padded] - part[:rows, padded:]
                out1[unit, peer, :, :padded] = real.astype(bf16)
                out1[unit, peer, :, padded:] = imag.astype(bf16)
            for peer in peers:

                @pl.when(peer != me)
                def _():
                    copy1(unit, peer).start()

        land1[unit, spot(me)] = out1[unit, me]

    def column_phase(unit):
        whole = land1.at[unit, pl.ds(0, (lat - 1) * rows)]
        pltpu.make_async_copy(whole, whole, recv1.at[unit]).wait()
        _, speed, base = scalars(unit)
        limit = (speed * base) ** 2
        lane = lax.broadcasted_iota(jnp.int32, (1, padded), 1) + me * width
        lane = jnp.where(lane < columns // 2, lane, lane - columns)
        column_wave = (2.0 * np.pi / columns) * lane.astype(f32)
        left = limit - column_wave * column_wave

        @pl.loop(0, lat // group)
        def _(turn_of):
            wide = jnp.dot(rowt[turn_of], land1[unit], preferred_element_type=f32)
            for place in range(group):
                part = wide[place * 2 * rows : (place + 1) * 2 * rows]
                block = turn_of * group + place
                real = part[:rows, :padded] + part[rows:, padded:]
                imag = part[:rows, padded:] - part[rows:, :padded]
                index = lax.broadcasted_iota(jnp.int32, (rows, 1), 0) + block * rows
                index = jnp.where(index < total_rows // 2, index, index - total_rows)
                row_wave = (2.0 * np.pi / total_rows) * index.astype(f32)
                square = left - row_wave * row_wave
                root = jnp.sqrt(jnp.abs(square)) * depth_step
                moving = square >= 0.0
                cosine = jnp.where(moving, series(COS_TERMS, square), jnp.exp(-root))
                sine = jnp.where(moving, root * series(SIN_TERMS, square), 0.0) * sign
                shifted[spot(block), :padded] = (real * cosine - imag * sine).astype(bf16)
                shifted[spot(block), padded:] = (imag * cosine + real * sine).astype(bf16)

        @pl.loop(0, lat // group)
        def _(step):
            turn_of = lax.rem(me // group + 1 + step, lat // group)
            wide = jnp.dot(rowt[turn_of], shifted[...], preferred_element_type=f32)
            for place in range(group):
                part = wide[place * 2 * rows : (place + 1) * 2 * rows]
                peer = turn_of * group + place
                real = part[:rows, :padded] - part[rows:, padded:]
                imag = part[:rows, padded:] + part[rows:, :padded]
                out2[unit, peer, :rows] = real.astype(bf16)
                out2[unit, peer, rows:] = imag.astype(bf16)

            for place in range(group):
                peer = turn_of * group + place

                @pl.when(peer != me)
                def _():
                    copy2(unit, peer).start()

        land2[unit, :, lane_spot(me)] = out2[unit, me]

    def row_inverse(unit):
        whole = land2.at[unit, :, pl.ds(0, (lat - 1) * padded)]
        pltpu.make_async_copy(whole, whole, recv2.at[unit]).wait()
        slab, speed, base = scalars(unit)
        scale = 1.0 / (total_rows * columns)
        slot = lax.rem(unit, 2)

        @pl.loop(0, y_blocks // 2)
        def _(pair):
            for block in (2 * pair, 2 * pair + 1):
                cols = pl.ds(pl.multiple_of(block * LANES, LANES), LANES)
                part = jnp.dot(land2[unit], inv[block], preferred_element_type=f32)
                real = part[:rows, :LANES] - part[rows:, LANES:]
                imag = part[rows:, :LANES] + part[:rows, LANES:]
                turn = depth_step * speed * (slow[slab, :, cols] - base)
                square = turn * turn
                cosine = series(COS_TERMS, square) * scale
                sine = turn * series(SIN_TERMS, square) * (sign * scale)
                new_real = real * cosine - imag * sine
                new_imag = imag * cosine + real * sine
                turned[slot, 0, 8 : 8 + rows, cols] = new_real
                turned[slot, 1, 8 : 8 + rows, cols] = new_imag
                halo_out[unit, 0, 0:1, cols] = new_real[0:1]
                halo_out[unit, 0, 1:2, cols] = new_imag[0:1]
                halo_out[unit, 1, 0:1, cols] = new_real[rows - 1 : rows]
                halo_out[unit, 1, 1:2, cols] = new_imag[rows - 1 : rows]

        @pl.when(me > 0)
        def _():
            halo_up(unit).start()

        @pl.when(me < lat - 1)
        def _():
            halo_down(unit).start()

    def finish(unit):
        @pl.when(me > 0)
        def _():
            halo_down(unit).wait_recv()

        @pl.when(me < lat - 1)
        def _():
            halo_up(unit).wait_recv()

        slab = unit // freqs
        slot = lax.rem(unit, 2)
        for plane in range(2):
            turned[slot, plane, 7:8] = halo_in[unit, 0, plane : plane + 1]
            turned[slot, plane, 8 + rows : 9 + rows] = halo_in[unit, 1, plane : plane + 1]
        lane = lax.broadcasted_iota(jnp.int32, (16, columns), 1)
        for start in range(0, rows, 16):
            middle, laps = [], []
            for plane in range(2):
                here = turned[slot, plane, 8 + start : 24 + start]
                above = turned[slot, plane, 7 + start : 23 + start]
                below = turned[slot, plane, 9 + start : 25 + start]
                left = jnp.where(lane == 0, 0.0, pltpu.roll(here, 1, 1))
                right = jnp.where(lane == columns - 1, 0.0, pltpu.roll(here, columns - 1, 1))
                middle.append(here)
                laps.append(above + below + left + right - 4.0 * here)
            weight = coef[slab, start : start + 16] * sign
            done[unit, 0, start : start + 16] = (middle[0] - weight * laps[1]).astype(bf16)
            done[unit, 1, start : start + 16] = (middle[1] + weight * laps[0]).astype(bf16)
        keep_copy(unit).start()
        pair_copy(unit).start()

    def look_up():
        @pl.loop(0, (columns // LANES) * 2)
        def _(index):
            slab = index // y_blocks
            block = index - slab * y_blocks
            cols = pl.ds(pl.multiple_of(block * LANES, LANES), LANES)
            here = bins[slab, :, cols]
            found_slow = jnp.zeros((rows, LANES), f32)
            found_coef = jnp.zeros((rows, LANES), f32)
            for level in range(bin_count):
                match = here == level
                found_slow = jnp.where(match, slow_table[slab, level], found_slow)
                found_coef = jnp.where(match, corr_table[slab, level], found_coef)
            slow[slab, :, cols] = found_slow
            coef[slab, :, cols] = found_coef

    @pl.loop(0, units + 3)
    def _(tick):
        @pl.when(tick >= 3)
        def _():
            finish(tick - 3)

        @pl.when(tick < units)
        def _():
            row_forward(tick)

        @pl.when(tick == 0)
        def _():
            loads[2].wait()
            loads[3].wait()
            loads[4].wait()
            look_up()

        @pl.when((tick >= 1) & (tick < units + 1))
        def _():
            column_phase(tick - 1)

        @pl.when((tick >= 2) & (tick < units + 2))
        def _():
            row_inverse(tick - 2)

    @pl.loop(0, units)
    def _(unit):
        sent1 = out1.at[unit, pl.ds(0, lat - 1)]
        pltpu.make_async_copy(sent1, sent1, send1.at[unit]).wait()
        sent2 = out2.at[unit, pl.ds(0, lat - 1)]
        pltpu.make_async_copy(sent2, sent2, send2.at[unit]).wait()

        @pl.when(me > 0)
        def _():
            halo_up(unit).wait_send()

        @pl.when(me < lat - 1)
        def _():
            halo_down(unit).wait_send()

        keep_copy(unit).wait()
        pltpu.make_async_remote_copy(
            src_ref=done.at[unit],
            dst_ref=out_hbm.at[1 - section, unit],
            send_sem=pair_send.at[unit],
            recv_sem=pair_recv.at[unit],
            device_id={"depth": 1 - section},
            device_id_type=MESH,
        ).wait()


def collect(freqs, picks, live, moved, image, fields, total):
    freq = pl.program_id(1)

    @pl.when(freq == 0)
    def _():
        total[...] = jnp.zeros_like(total)

    @pl.when(live[freq] > 0)
    def _():
        fields[0, 0, 0:2] = moved[0, 0]
        fields[0, 0, 2:4] = moved[1, 0]
        source = moved[0, 0].astype(f32)
        receiver = moved[1, 0].astype(f32)
        total[...] += source[0] * receiver[0] + source[1] * receiver[1]

    @pl.when(live[freq] == 0)
    def _():
        fields[...] = jnp.zeros_like(fields)

    @pl.when(freq == freqs - 1)
    def _():
        image[0] = total[...].astype(image.dtype)


def per_device(
    fwd_table,
    row_table,
    inv_table,
    wavefields,
    angular_freq,
    base_slowness,
    slow_table,
    correction_table,
    velocity_bins,
    last_slab,
):
    freqs, _, rows, columns = wavefields.shape
    slabs, bin_count = slow_table.shape
    lat = lax.axis_size("lat")
    section = lax.axis_index("depth")
    width = columns // lat
    padded = max(LANES, width)
    continued = last_slab > 1
    order = jnp.arange(freqs, dtype=jnp.int32)
    key = jnp.where(continued, order, order + freqs)
    rank = jnp.sum((key[None, :] < key[:, None]).astype(jnp.int32), axis=1)
    perm = jnp.sum(jnp.where(rank[None, :] == order[:, None], order[None, :], 0), axis=1)
    count = jnp.sum(continued.astype(jnp.int32))
    live = (section < last_slab).astype(jnp.int32)

    def branch(number):
        units = freqs + number
        sizes = (freqs, units, lat, rows, columns, width, padded, bin_count)
        smem = pl.BlockSpec(memory_space=pltpu.SMEM)
        hbm = pl.BlockSpec(memory_space=pl.ANY)
        chunk = (units, lat, rows, 2 * padded)
        moved = pl.pallas_call(
            functools.partial(migrate, sizes),
            out_shape=jax.ShapeDtypeStruct((2, units, 2, rows, columns), bf16),
            in_specs=[smem] * 5 + [hbm] * 5,
            out_specs=hbm,
            scratch_shapes=[
                pltpu.VMEM((freqs, 2, rows, columns), bf16),
                pltpu.VMEM((slabs, rows, columns), jnp.int32),
                pltpu.VMEM(fwd_table.shape, bf16),
                pltpu.VMEM(row_table.shape, bf16),
                pltpu.VMEM(inv_table.shape, bf16),
                pltpu.VMEM((slabs, rows, columns), f32),
                pltpu.VMEM((slabs, rows, columns), f32),
                pltpu.VMEM((2 * rows, columns), bf16),
                pltpu.VMEM(chunk, bf16),
                pltpu.VMEM((units, rows * lat, 2 * padded), bf16),
                pltpu.VMEM((rows * lat, 2 * padded), bf16),
                pltpu.VMEM((units, lat, 2 * rows, padded), bf16),
                pltpu.VMEM((units, 2 * rows, lat * padded), bf16),
                pltpu.VMEM((2, 2, rows + 16, columns), f32),
                pltpu.VMEM((units, 2, 8, columns), f32),
                pltpu.VMEM((units, 2, 8, columns), f32),
                pltpu.VMEM((units, 2, rows, columns), bf16),
                pltpu.SemaphoreType.DMA((5,)),
                pltpu.SemaphoreType.DMA((units,)),
                pltpu.SemaphoreType.DMA((units,)),
                pltpu.SemaphoreType.DMA((units,)),
                pltpu.SemaphoreType.DMA((units,)),
                pltpu.SemaphoreType.DMA((units, 2)),
                pltpu.SemaphoreType.DMA((units, 2)),
                pltpu.SemaphoreType.DMA((units,)),
                pltpu.SemaphoreType.DMA((units,)),
                pltpu.SemaphoreType.DMA((units,)),
            ],
            compiler_params=pltpu.CompilerParams(
                collective_id=number - 1, has_side_effects=True, vmem_limit_bytes=62 * 2**20
            ),
            name=f"migrate_{units}",
        )(
            perm,
            angular_freq,
            base_slowness,
            slow_table,
            correction_table,
            wavefields,
            velocity_bins,
            fwd_table,
            row_table,
            inv_table,
        )
        picks = jnp.where(section == 0, rank, jnp.minimum(freqs + rank, units - 1))
        tile = rows
        return pl.pallas_call(
            functools.partial(collect, freqs),
            out_shape=(
                jax.ShapeDtypeStruct((1, rows, columns), bf16),
                jax.ShapeDtypeStruct((1, freqs, 4, rows, columns), bf16),
            ),
            grid_spec=pltpu.PrefetchScalarGridSpec(
                num_scalar_prefetch=2,
                grid=(rows // tile, freqs),
                in_specs=[
                    pl.BlockSpec((2, 1, 2, tile, columns), lambda r, f, picks, live: (0, picks[f], 0, r, 0))
                ],
                out_specs=[
                    pl.BlockSpec((1, tile, columns), lambda r, f, picks, live: (0, r, 0)),
                    pl.BlockSpec((1, 1, 4, tile, columns), lambda r, f, picks, live: (0, f, 0, r, 0)),
                ],
                scratch_shapes=[pltpu.VMEM((tile, columns), f32)],
            ),
            name=f"collect_{units}",
        )(picks, live, moved)

    picked = jnp.clip(count - 1, 0, freqs - 2)
    return lax.switch(picked, [functools.partial(branch, number) for number in range(1, freqs)])


def solution(mesh):
    lat = mesh.shape["lat"]
    in_specs = (
        P(),
        P(),
        P(),
        P("shot", None, "lat", None),
        P(),
        P(),
        P(),
        P(),
        P(None, "lat", None),
        P(),
    )
    out_specs = (P(("shot", "depth"), "lat", None), P(("shot", "depth"), None, None, "lat", None))
    body = jax.shard_map(
        per_device, mesh=mesh, in_specs=in_specs, out_specs=out_specs, check_vma=False
    )

    def run(wavefields, *rest):
        total_rows, columns = wavefields.shape[2:]
        padded = max(LANES, columns // lat)
        cosine_x, sine_x = wave_tables(total_rows)
        cosine_y, sine_y = wave_tables(columns)
        return body(
            jnp.asarray(forward_blocks(cosine_y, sine_y, lat, padded)),
            jnp.asarray(row_blocks(cosine_x, sine_x, lat)),
            jnp.asarray(inverse_blocks(cosine_y, sine_y, lat, padded)),
            wavefields,
            *rest,
        )

    return run
```
